128 devices in a mesh: lon: 8 (over y, core), lat: 16 (over x, z).
Axes of the slice: x: 4, y: 4, z: 4, core: 2. Of those that a mesh axis runs over, the one named last changes fastest.
Arguments:
- tangent: float32 [5, 72, 16, 9216], P(None, None, 'lat', 'lon'), may hold values from -6 to 6
- adjoint: float32 [5, 72, 16, 9216], P(None, None, 'lat', 'lon'), may hold values from -6 to 6
- winds: float32 [2, 72, 16, 9216], P(None, None, 'lat', 'lon'), may hold values from -3 to 3
- cutoff: int32 [128], replicated, may hold values from 72 to 576, as said below
Outputs:
- tl_out: float32 [5, 72, 16, 9216], P(None, None, 'lat', 'lon')
- adj_out: float32 [5, 72, 16, 9216], P(None, None, 'lat', 'lon')
The draws below stay inside these ranges and needn't reach their ends.
Inputs may be any that keep to these rules, and one draw needn't show every extreme that they name: `cutoff`: rows j with 32 <= j < 96 hold values from 288 to 576, and row 64 holds 576; the other rows hold values from 72 to 575, and row 0 holds 72.
All inputs are finite; a program needn't handle non-finite values.
Results may differ from the reference program's by a relative error of at most 0.00008.
Values sent between devices are 32-bit elements; how exact they have to be, the bound alone decides.
A program may use at most 128 MiB of HBM per device.

```python
import jax
import jax.numpy as jnp

NLON = 1152
FIELDS = 5
LEV = 72
ROWS = 8
NLAT = 128
NLOC = 144
N_LON = 8
N_LAT = 16


def draw_cutoff(key, part):
    key = jax.random.fold_in(key, 11)
    row = jnp.arange(NLAT, dtype=jnp.int32)
    polar_key, middle_key = jax.random.split(key)
    drawn = jax.random.randint(polar_key, (NLAT,), NLON // 16, NLON // 2, dtype=jnp.int32)
    drawn = jnp.where(row == 0, NLON // 16, drawn)
    middle = jax.random.randint(middle_key, (NLAT,), NLON // 4, NLON // 2 + 1, dtype=jnp.int32)
    middle = jnp.where(row == NLAT // 2, NLON // 2, middle)
    polar = (row < NLAT // 4) | (row >= NLAT - NLAT // 4)
    return jnp.where(polar, drawn, middle).astype(jnp.int32)


def shard_levels(key, extent, cuts, least, top_value):
    factor_of = 1.0
    for axis_at, shards_of in cuts:
        draws = jax.random.uniform(jax.random.fold_in(jax.random.fold_in(key, 6), axis_at), (shards_of,), jnp.float32, least / len(cuts), top_value / len(cuts))
        factor_of = factor_of * jnp.repeat(jnp.exp(draws), extent[axis_at] // shards_of).reshape((-1,) + (1,) * (len(extent) - 1 - axis_at))
    return factor_of


def scatter_about(stream_key, shape, width, most, shards=(), kind=jnp.bfloat16):
    array = jax.random.normal(stream_key, shape, jnp.float32) * width
    if len(shards) > 0:
        array = shard_levels(stream_key, shape, shards, -0.22, 0.18) * array
    return jnp.clip(array, min=-most, max=most).astype(kind)


def setup_inputs(seed: int = 0) -> dict:
    key_list = jax.random.split(jax.random.key(seed), 5)
    return {
        "tangent": scatter_about(key_list[0], (FIELDS, LEV, N_LAT, N_LON * ROWS * NLOC), 1.0, 6.0, ((2, 16), (3, 8)), jnp.float32),
        "adjoint": scatter_about(key_list[1], (FIELDS, LEV, N_LAT, N_LON * ROWS * NLOC), 1.0, 6.0, ((2, 16), (3, 8)), jnp.float32),
        "winds": scatter_about(key_list[2], (2, LEV, N_LAT, N_LON * ROWS * NLOC), 0.5, 3.0, ((2, 16), (3, 8)), jnp.float32),
        "cutoff": draw_cutoff(jax.random.fold_in(key_list[4], 71), 0),
    }


def to_grid(blocked):
    lead = blocked.shape[:-2]
    split = blocked.reshape(lead + (N_LAT, N_LON, ROWS, NLOC))
    split = jnp.swapaxes(split, -3, -2)
    return split.reshape(lead + (N_LAT * ROWS, N_LON * NLOC))


def to_blocks(field):
    lead = field.shape[:-2]
    split = field.reshape(lead + (N_LAT, ROWS, N_LON, NLOC))
    split = jnp.swapaxes(split, -3, -2)
    return split.reshape(lead + (N_LAT, N_LON * ROWS * NLOC))


def gains(limit, nring):
    wave = jnp.arange(nring // 2 + 1).astype(jnp.float32)
    bound = limit.astype(jnp.float32)[:, None]
    ratio = bound / jnp.maximum(wave, 1.0)[None, :]
    return jnp.where(wave[None, :] <= bound, 1.0, ratio * ratio).astype(jnp.float32)


def advance(field_pad, east_pad, north_pad):
    face_east = east_pad[:, 1:-1, :-1] * (field_pad[..., 1:-1, :-1] + field_pad[..., 1:-1, 1:]) * 0.5
    face_north = north_pad[:, :-1, 1:-1] * (field_pad[..., :-1, 1:-1] + field_pad[..., 1:, 1:-1]) * 0.5
    inner = field_pad[..., 1:-1, 1:-1]
    return inner - (face_east[..., 1:] - face_east[..., :-1]) - (face_north[..., 1:, :] - face_north[..., :-1, :])


def retreat(field_pad, east_pad, north_pad):
    face_east = east_pad[:, 1:-1, :-1] * (field_pad[..., 1:-1, :-1] - field_pad[..., 1:-1, 1:]) * 0.5
    face_north = north_pad[:, :-1, 1:-1] * (field_pad[..., :-1, 1:-1] - field_pad[..., 1:, 1:-1]) * 0.5
    inner = field_pad[..., 1:-1, 1:-1]
    return inner - (face_east[..., 1:] + face_east[..., :-1]) - (face_north[..., 1:, :] + face_north[..., :-1, :])


def pad_field(field):
    field = jnp.concatenate([field[..., -1:], field, field[..., :1]], axis=-1)
    zero = jnp.zeros_like(field[..., :1, :])
    return jnp.concatenate([zero, field, zero], axis=-2)


def damp(field, gain):
    spectrum = jnp.fft.rfft(field, axis=-1)
    return jnp.fft.irfft(spectrum * gain, n=NLON, axis=-1).astype(field.dtype)


def reference(tangent, adjoint, winds, cutoff):
    tangent = to_grid(tangent)
    adjoint = to_grid(adjoint)
    winds = to_grid(winds)
    gain = gains(cutoff, NLON)
    row = jnp.arange(NLAT + 2, dtype=jnp.int32) - 1
    valid = ((row >= 0) & (row <= NLAT - 2)).astype(jnp.float32)
    east_pad = pad_field(winds[0])
    north_pad = pad_field(winds[1]) * valid[None, :, None]
    moved = advance(pad_field(tangent), east_pad, north_pad)
    tl_out = damp(moved, gain)
    damped = damp(adjoint, gain)
    adj_out = retreat(pad_field(damped), east_pad, north_pad)
    return to_blocks(tl_out), to_blocks(adj_out)
```

```python
import functools
import math

import jax
import jax.numpy as jnp
import numpy as np
from jax import lax
from jax.experimental import pallas as pl
from jax.experimental.pallas import tpu as pltpu
from jax.sharding import PartitionSpec as P

MESH = pl.DeviceIdType.MESH
F32 = jnp.float32
BF16 = jnp.bfloat16
ROWS = 8
PIECES = 8
LANES = 128
BLOCK = 256
SPAN = 512
KINDS = (0, 4, 1, 2, 3)
ORDER = (4, 3, 5, 2, 6, 1, 7)
ROOT = math.sqrt(0.5)


def split_table(nring):
    lag = np.arange(SPAN) - SPAN // 2
    count = nring // PIECES
    parts = []
    for kind in KINDS:
        wave = kind + PIECES * np.arange(count)
        angle = (wave[:, None] * lag[None, :] % nring) * (2.0 * np.pi / nring)
        forms = (np.cos,) if kind in (0, 4) else (np.cos, np.sin)
        weight = (1.0 if kind in (0, 4) else 2.0) / nring
        for form in forms:
            parts.append(weight * form(angle))
    return np.stack(parts).astype(np.float32)


def halves(value):
    high = value.astype(BF16)
    return high, (value - high.astype(F32)).astype(BF16)


def dot(a, b):
    return jnp.dot(a, b, preferred_element_type=F32)


def to_parts(x):
    s0, d0 = x[0] + x[4], x[0] - x[4]
    s1, d1 = x[1] + x[5], x[1] - x[5]
    s2, d2 = x[2] + x[6], x[2] - x[6]
    s3, d3 = x[3] + x[7], x[3] - x[7]
    even, odd = s0 + s2, s1 + s3
    p, q = (d1 - d3) * ROOT, (d1 + d3) * ROOT
    return (even + odd, even - odd, d0 + p, -d2 - q, s0 - s2, s3 - s1, d0 - p, d2 - q)


def from_parts(z):
    a, b = z[0] + z[1], z[0] - z[1]
    even = (a + z[4], b - z[5], a - z[4], b + z[5])
    p, q = (z[2] - z[6]) * ROOT, (z[3] + z[7]) * ROOT
    odd = (z[2] + z[6], p - q, z[7] - z[3], -p - q)
    return [e + o for e, o in zip(even, odd)] + [e - o for e, o in zip(even, odd)]


def kernel(
    dims,
    cut_ref,
    table_hbm,
    tan_hbm,
    adj_hbm,
    wind_hbm,
    tl_out,
    adj_out,
    tan_v,
    wind_v,
    moved_v,
    damped_v,
    result_v,
    got_a,
    got_t,
    back_a,
    back_t,
    south_t,
    north_t,
    south_d,
    north_d,
    south_w,
    wind_row,
    line_t,
    line_d,
    edge_t,
    edge_d,
    table_v,
    lag_v,
    mat_high,
    mat_low,
    part_high,
    part_low,
    image_v,
    local_sem,
    fwd_a_send,
    fwd_a_recv,
    fwd_t_send,
    fwd_t_recv,
    back_a_send,
    back_a_recv,
    back_t_send,
    back_t_recv,
    edge_send,
    edge_recv,
    row_send,
    row_recv,
):
    fields, levels, share, slot = dims
    chans = fields * levels
    groups = levels // 8
    tiles = ROWS * 144 // LANES
    size, room = share * tiles, slot * tiles
    me = lax.axis_index("lon")
    band = lax.axis_index("lat")
    bands = lax.axis_size("lat")
    west, east = lax.rem(me + PIECES - 1, PIECES), lax.rem(me + 1, PIECES)
    south, north = lax.rem(band + bands - 1, bands), lax.rem(band + 1, bands)
    lane = lax.broadcasted_iota(jnp.int32, (8, LANES), 1)
    in16 = lane % 16
    sub = lane // 16

    barrier = pltpu.get_barrier_semaphore()
    for step in range(1, PIECES):
        pl.semaphore_signal(
            barrier, inc=1, device_id={"lon": lax.rem(me + step, PIECES)}, device_id_type=MESH
        )
    for other in (south, north):
        pl.semaphore_signal(barrier, inc=1, device_id={"lat": other}, device_id_type=MESH)

    load_tan = pltpu.make_async_copy(tan_hbm, tan_v, local_sem.at[0])
    load_wind = pltpu.make_async_copy(wind_hbm, wind_v, local_sem.at[1])
    load_table = pltpu.make_async_copy(table_hbm, table_v, local_sem.at[2])
    own_a = pltpu.make_async_copy(
        adj_hbm.at[pl.ds(me * size, size)], got_a.at[pl.ds(me * room, size)], local_sem.at[4]
    )
    load_tan.start()
    load_wind.start()
    own_a.start()
    load_table.start()

    def tile_of(ref, row, stride=tiles, count=8):
        return ref[pl.ds(row, count, stride=stride), :]

    def pack(source, wind, edge, line):
        planes = fields + (1 if wind is not None else 0)

        def body(lg, carry):
            first, last = list(carry[0]), list(carry[1])
            for f in range(planes):
                if f < fields:
                    at = (f * groups + lg) * 8
                    t = [tile_of(source, at * tiles + k) for k in range(tiles)]
                    for k in range(2):
                        line[0, pl.ds(k * chans + at, 8), :] = t[k]
                        line[1, pl.ds(k * chans + at, 8), :] = t[k + tiles - 2]
                else:
                    t = [tile_of(wind, lg * 8 * tiles + k) for k in range(tiles)]
                    for k in range(2):
                        wind_row[pl.ds(k * levels + lg * 8, 8), :] = tile_of(
                            wind, (groups + lg) * 8 * tiles + k + tiles - 2
                        )
                a, b = t[0], t[1]
                for r in range(1, ROWS):
                    a = jnp.where(sub == r, t[r], a)
                    b = jnp.where(sub == r, t[r + 1], b)
                here = in16 == lg
                first[f] = jnp.where(here, pltpu.roll(a, lg, 1), first[f])
                last[f] = jnp.where(here, pltpu.roll(b, lg + (LANES - 15), 1), last[f])
            return tuple(first), tuple(last)

        zero = tuple(jnp.zeros((8, LANES), F32) for _ in range(planes))
        first, last = lax.fori_loop(0, groups, body, (zero, zero))
        for f in range(planes):
            edge[0, 8 * f : 8 * f + 8, :] = first[f]
            edge[1, 8 * f : 8 * f + 8, :] = last[f]

    def edges(edge, at):
        return [
            pltpu.make_async_remote_copy(
                edge.at[0], edge.at[3], edge_send.at[at, 0], edge_recv.at[at, 0],
                device_id={"lon": west}, device_id_type=MESH,
            ),
            pltpu.make_async_remote_copy(
                edge.at[1], edge.at[2], edge_send.at[at, 1], edge_recv.at[at, 1],
                device_id={"lon": east}, device_id_type=MESH,
            ),
        ]

    def rows(line, to_south, to_north, at):
        return [
            pltpu.make_async_remote_copy(
                line.at[0], to_south, row_send.at[at, 0], row_recv.at[at, 0],
                device_id={"lat": south}, device_id_type=MESH,
            ),
            pltpu.make_async_remote_copy(
                line.at[1], to_north, row_send.at[at, 1], row_recv.at[at, 1],
                device_id={"lat": north}, device_id_type=MESH,
            ),
        ]

    def stencil(source, edge, from_south, from_north, target, sign):
        has_south = jnp.where(band > 0, 0.5, 0.0).astype(F32)
        has_north = jnp.where(band < bands - 1, 0.5, 0.0).astype(F32)

        def left(x, n):
            return pltpu.roll(x, LANES - n, 1)

        def body(lg, _):
            u = [tile_of(wind_v, lg * 8 * tiles + k) * 0.5 for k in range(tiles)]
            v = [tile_of(wind_v, (groups + lg) * 8 * tiles + k) for k in range(tiles)]
            v = [x * 0.5 for x in v[:-2]] + [v[-2] * jnp.where(lane >= 112, has_north, 0.5), v[-1] * has_north]
            v = [south_w[pl.ds(k * levels + lg * 8, 8), :] * has_south for k in range(2)] + v
            u_west = pltpu.roll(edge_t[2, 8 * fields : 8 * fields + 8, :], LANES - lg, 1) * 0.5
            for f in range(fields):
                at = (f * groups + lg) * 8
                t = [tile_of(source, at * tiles + k) for k in range(tiles)]
                far_west = pltpu.roll(edge[2, 8 * f : 8 * f + 8, :], LANES - lg, 1)
                far_east = pltpu.roll(edge[3, 8 * f : 8 * f + 8, :], 15 - lg, 1)
                shifted = [left(x, 1) for x in t]
                flux = []
                for k in range(tiles):
                    nxt = jnp.where(lane == 127, shifted[k + 1], shifted[k]) if k + 1 < tiles else shifted[k]
                    if k >= 1:
                        nxt = jnp.where(lane == 16 * (k - 1) + 15, far_east, nxt)
                    flux.append(u[k] * (t[k] + sign * nxt))
                turned = [pltpu.roll(x, 1, 1) for x in flux]
                out = []
                for k in range(tiles):
                    prev = jnp.where(lane == 0, turned[k - 1], turned[k]) if k >= 1 else turned[k]
                    if k < ROWS:
                        prev = jnp.where(lane == 16 * k, u_west * (far_west + sign * t[k]), prev)
                    out.append(t[k] - flux[k] + sign * prev)
                ext = [from_south[pl.ds(k * chans + at, 8), :] for k in range(2)] + t
                ext = ext + [from_north[pl.ds(k * chans + at, 8), :] for k in range(2)]
                shifted = [left(x, 16) for x in ext]
                flux = []
                for k in range(tiles + 2):
                    nxt = jnp.where(lane < 112, shifted[k + 1], shifted[k + 2])
                    flux.append(v[k] * (ext[k] + sign * nxt))
                turned = [pltpu.roll(x, 16, 1) for x in flux]
                for k in range(tiles):
                    prev = jnp.where(lane >= 16, turned[k + 1], turned[k])
                    target[pl.ds(at * tiles + k, 8, stride=tiles), :] = out[k] - flux[k + 2] + sign * prev
            return 0

        lax.fori_loop(0, groups, body, 0)

    def matrices():
        grow = lax.broadcasted_iota(jnp.int32, (8, 144), 0)
        limit = jnp.zeros((8, 144), F32)
        for r in range(ROWS):
            limit = jnp.where(grow == r, cut_ref[band * ROWS + r].astype(F32), limit)
        column = lax.broadcasted_iota(jnp.int32, (8, 144), 1)
        nring = PIECES * 144
        part = 0
        for kind in KINDS:
            wave = column * PIECES + kind
            wave = jnp.minimum(wave, jnp.abs(nring - wave)).astype(F32)
            ratio = limit / jnp.maximum(wave, 1.0)
            gain = jnp.where(wave <= limit, 1.0, ratio * ratio)
            high, low = halves(gain)
            both = jnp.concatenate([high, low], axis=0)
            for _ in range(1 if kind in (0, 4) else 2):
                table_high, table_low = halves(table_v[part])
                one = dot(both, table_high)
                two = dot(both, table_low)
                lag_v[part] = one[:8] + one[8:] + two[:8]
                part += 1

        wide = lax.broadcasted_iota(jnp.int32, (16, BLOCK), 1)

        def body(r, _):
            inside = (wide >= 16 * r) & (wide < 16 * r + 144)
            nought = jnp.zeros((16, PIECES * BLOCK), BF16)
            for a in range(9, 16):
                row = lax.rem(r + a, 16) * 16
                mat_high[r, pl.ds(row, 16), :] = nought
                mat_low[r, pl.ds(row, 16), :] = nought
            for part in range(PIECES):
                line = jnp.broadcast_to(lag_v[part, pl.ds(r, 1), :], (16, SPAN))
                strip = pltpu.roll(line, 0, 1, stride=1, stride_axis=0)
                strip = pltpu.roll(strip, 16 * r + (SPAN - 128), 1)
                for a in range(9):
                    block = jnp.where(inside, strip[:, 128 - 16 * a : 384 - 16 * a], 0.0)
                    high, low = halves(block)
                    row = (r + a) * 16
                    mat_high[r, pl.ds(row, 16), part * BLOCK : (part + 1) * BLOCK] = high
                    mat_low[r, pl.ds(row, 16), part * BLOCK : (part + 1) * BLOCK] = low
            return 0

        lax.fori_loop(0, ROWS, body, 0)

    def damp(got, back):
        def forward(p, _):
            for t in range(tiles):
                x = [got[pl.ds(c * room + p * 16 * tiles + t, 16, stride=tiles), :] for c in range(PIECES)]
                for k, y in enumerate(to_parts(x)):
                    high, low = halves(y)
                    part_high[k, pl.ds(p * 16, 16), t * LANES : (t + 1) * LANES] = high
                    part_low[k, pl.ds(p * 16, 16), t * LANES : (t + 1) * LANES] = low
            return 0

        lax.fori_loop(0, slot // 16, forward, 0)
        image_v[:, :, 0:LANES] = jnp.zeros((PIECES, slot, LANES), F32)

        def multiply(r, _):
            window = pl.ds(pl.multiple_of(r * LANES, LANES), BLOCK)
            this = pl.ds(pl.multiple_of(r * LANES, LANES), LANES)
            following = pl.ds(pl.multiple_of(r * LANES + LANES, LANES), LANES)

            def product(first, count):
                high = part_high[first : first + count, :, window].reshape(count * slot, BLOCK)
                low = part_low[first : first + count, :, window].reshape(count * slot, BLOCK)
                cols = slice(first * BLOCK, (first + count) * BLOCK)
                wide_high, wide_low = mat_high[r, :, cols], mat_low[r, :, cols]
                return dot(high, wide_high) + dot(low, wide_high) + dot(high, wide_low)

            def put(k, z):
                image_v[k, :, this] = image_v[k, :, this] + z[:, :LANES]
                image_v[k, :, following] = z[:, LANES:]

            put(0, product(0, 1))
            put(1, product(1, 1))
            for k in (2, 4, 6):
                z = product(k, 2)
                put(k, z[:slot, :BLOCK] - z[slot:, BLOCK:])
                put(k + 1, z[:slot, BLOCK:] + z[slot:, :BLOCK])
            return 0

        lax.fori_loop(0, ROWS, multiply, 0)

        def inverse(p, _):
            for t in range(tiles):
                z = [image_v[k, pl.ds(p * 8, 8), t * LANES : (t + 1) * LANES] for k in range(PIECES)]
                for c, x in enumerate(from_parts(z)):
                    back[pl.ds(c * room + p * 8 * tiles + t, 8, stride=tiles), :] = x
            return 0

        lax.fori_loop(0, slot // 8, inverse, 0)

    def scatter(source, got, send, recv):
        out = []
        for step in ORDER:
            to = lax.rem(me + step, PIECES)
            out.append(
                pltpu.make_async_remote_copy(
                    source.at[pl.ds(to * size, size)], got.at[pl.ds(me * room, size)],
                    send.at[step], recv.at[step], device_id={"lon": to}, device_id_type=MESH,
                )
            )
        return out

    def bring(back, target, send, recv):
        out = []
        for step in ORDER:
            to = lax.rem(me + step, PIECES)
            out.append(
                pltpu.make_async_remote_copy(
                    back.at[pl.ds(to * room, size)], target.at[pl.ds(me * size, size)],
                    send.at[step], recv.at[step], device_id={"lon": to}, device_id_type=MESH,
                )
            )
        return out

    def start(copies):
        for c in copies:
            c.start()

    def wait_recv(copies):
        for c in copies:
            c.wait_recv()

    def wait_send(copies):
        for c in copies:
            c.wait_send()

    load_tan.wait()
    load_wind.wait()
    pack(
        tan_v, wind_v, edge_t, line_t
    )
    pl.semaphore_wait(barrier, PIECES + 1)

    edges_t = edges(edge_t, 0)
    start(edges_t)
    send_a = scatter(adj_hbm, got_a, fwd_a_send, fwd_a_recv)
    start(send_a)
    rows_t = rows(line_t, north_t, south_t, 0)
    rows_w = pltpu.make_async_remote_copy(
        wind_row, south_w,
        row_send.at[2, 0], row_recv.at[2, 0], device_id={"lat": north}, device_id_type=MESH,
    )
    start(rows_t)
    rows_w.start()

    load_table.wait()
    matrices()

    wait_recv(edges_t)
    wait_recv(rows_t)
    rows_w.wait_recv()
    stencil(tan_v, edge_t, south_t, north_t, moved_v, 1.0)
    send_t = scatter(moved_v, got_t, fwd_t_send, fwd_t_recv)
    start(send_t)
    own_t = pltpu.make_async_copy(
        moved_v.at[pl.ds(me * size, size)], got_t.at[pl.ds(me * room, size)], local_sem.at[5]
    )
    own_t.start()

    own_a.wait()
    wait_recv(send_a)
    damp(got_a, back_a)
    home_a = bring(back_a, damped_v, back_a_send, back_a_recv)
    start(home_a)
    keep_a = pltpu.make_async_copy(
        back_a.at[pl.ds(me * room, size)], damped_v.at[pl.ds(me * size, size)], local_sem.at[6]
    )
    keep_a.start()

    own_t.wait()
    wait_recv(send_t)
    damp(got_t, back_t)

    keep_a.wait()
    wait_recv(home_a)
    pack(damped_v, None, edge_d, line_d)
    edges_d = edges(edge_d, 1)
    start(edges_d)
    rows_d = rows(line_d, north_d, south_d, 1)
    start(rows_d)
    home_t = bring(back_t, tl_out, back_t_send, back_t_recv)
    start(home_t)
    keep_t = pltpu.make_async_copy(
        back_t.at[pl.ds(me * room, size)], tl_out.at[pl.ds(me * size, size)], local_sem.at[7]
    )
    keep_t.start()

    wait_recv(edges_d)
    wait_recv(rows_d)
    stencil(damped_v, edge_d, south_d, north_d, result_v, -1.0)
    store = pltpu.make_async_copy(result_v, adj_out, local_sem.at[8])
    store.start()

    for copies in (edges_t, send_a, rows_t, send_t, home_a, edges_d, rows_d):
        wait_send(copies)
    rows_w.wait_send()
    keep_t.wait()
    store.wait()
    for c in home_t:
        c.wait()


def shards(tangent, adjoint, winds, cutoff):
    fields, levels, single, cells = tangent.shape
    chans = fields * levels
    share = chans // PIECES
    slot = -(-share // 16) * 16
    tiles = cells // LANES
    table = split_table(PIECES * cells // ROWS)
    state = jax.ShapeDtypeStruct((chans * tiles, LANES), F32)
    any_space = pl.BlockSpec(memory_space=pl.ANY)
    vmem = pltpu.VMEM
    dma = pltpu.SemaphoreType.DMA
    whole = vmem((chans * tiles, LANES), F32)
    tl, adj = pl.pallas_call(
        functools.partial(kernel, (fields, levels, share, slot)),
        out_shape=(state, state),
        in_specs=[pl.BlockSpec(memory_space=pltpu.SMEM)] + [any_space] * 4,
        out_specs=(any_space, any_space),
        scratch_shapes=[
            whole,
            vmem((2 * levels * tiles, LANES), F32),
            whole,
            whole,
            whole,
            *[vmem((PIECES * slot * tiles, LANES), F32)] * 4,
            *[vmem((2 * chans, LANES), F32)] * 4,
            *[vmem((2 * levels, LANES), F32)] * 2,
            *[vmem((2, 2 * chans, LANES), F32)] * 2,
            vmem((4, 8 * (fields + 1), LANES), F32),
            vmem((4, 8 * fields, LANES), F32),
            vmem((PIECES, 144, SPAN), F32),
            vmem((PIECES, ROWS, SPAN), F32),
            vmem((ROWS, BLOCK, PIECES * BLOCK), BF16),
            vmem((ROWS, BLOCK, PIECES * BLOCK), BF16),
            vmem((PIECES, slot, cells), BF16),
            vmem((PIECES, slot, cells), BF16),
            vmem((PIECES, slot, cells), F32),
            dma((9,)),
            *[dma((PIECES,))] * 8,
            dma((2, 2)),
            dma((2, 2)),
            dma((3, 2)),
            dma((3, 2)),
        ],
        compiler_params=pltpu.CompilerParams(
            collective_id=0, has_side_effects=True, vmem_limit_bytes=60 * 1024 * 1024
        ),
    )(
        cutoff,
        jnp.asarray(table),
        tangent.reshape(chans * tiles, LANES),
        adjoint.reshape(chans * tiles, LANES),
        winds.reshape(2 * levels * tiles, LANES),
    )
    return tl.reshape(tangent.shape), adj.reshape(tangent.shape)


def solution(mesh):
    band = P(None, None, "lat", "lon")
    return jax.shard_map(
        shards, mesh=mesh, in_specs=(band, band, band, P()), out_specs=(band, band), check_vma=False
    )
```

```python
import functools
import math

import jax
import jax.numpy as jnp
import numpy as np
from jax import lax
from jax.experimental import pallas as pl
from jax.experimental.pallas import tpu as pltpu
from jax.sharding import PartitionSpec as P

MESH = pl.DeviceIdType.MESH
F32 = jnp.float32
BF16 = jnp.bfloat16
ROWS = 8
PIECES = 8
LANES = 128
BLOCK = 256
SPAN = 512
KINDS = (0, 4, 1, 2, 3)
ORDER = (4, 3, 5, 2, 6, 1, 7)
FIRST = 2
PARTS = 1
ROOT = math.sqrt(0.5)


def split_table(nring):
    lag = np.arange(SPAN) - SPAN // 2
    count = nring // PIECES
    parts = []
    for kind in KINDS:
        wave = kind + PIECES * np.arange(count)
        angle = (wave[:, None] * lag[None, :] % nring) * (2.0 * np.pi / nring)
        forms = (np.cos,) if kind in (0, 4) else (np.cos, np.sin)
        weight = (1.0 if kind in (0, 4) else 2.0) / nring
        for form in forms:
            parts.append(weight * form(angle))
    return np.stack(parts).astype(np.float32)


def halves(value):
    high = value.astype(BF16)
    return high, (value - high.astype(F32)).astype(BF16)


def dot(a, b):
    return jnp.dot(a, b, preferred_element_type=F32)


def to_parts(x):
    s0, d0 = x[0] + x[4], x[0] - x[4]
    s1, d1 = x[1] + x[5], x[1] - x[5]
    s2, d2 = x[2] + x[6], x[2] - x[6]
    s3, d3 = x[3] + x[7], x[3] - x[7]
    even, odd = s0 + s2, s1 + s3
    p, q = (d1 - d3) * ROOT, (d1 + d3) * ROOT
    return (even + odd, even - odd, d0 + p, -d2 - q, s0 - s2, s3 - s1, d0 - p, d2 - q)


def from_parts(z):
    a, b = z[0] + z[1], z[0] - z[1]
    even = (a + z[4], b - z[5], a - z[4], b + z[5])
    p, q = (z[2] - z[6]) * ROOT, (z[3] + z[7]) * ROOT
    odd = (z[2] + z[6], p - q, z[7] - z[3], -p - q)
    return [e + o for e, o in zip(even, odd)] + [e - o for e, o in zip(even, odd)]


def kernel(
    dims,
    cut_ref,
    table_hbm,
    tan_hbm,
    adj_hbm,
    wind_hbm,
    tl_out,
    adj_out,
    tan_v,
    wind_v,
    moved_v,
    damped_v,
    got_a,
    got_t,
    back_a,
    back_t,
    south_t,
    north_t,
    south_d,
    north_d,
    south_w,
    wind_row,
    line_t,
    line_d,
    edge_t,
    edge_d,
    table_v,
    lag_v,
    mat_high,
    mat_low,
    part_high,
    part_low,
    image_v,
    local_sem,
    fwd_a_send,
    fwd_a_recv,
    fwd_t_send,
    fwd_t_recv,
    back_a_send,
    back_a_recv,
    back_t_send,
    back_t_recv,
    edge_send,
    edge_recv,
    row_send,
    row_recv,
    cycle_sem,
    bands_sem,
):
    fields, levels, share, slot = dims
    chans = fields * levels
    groups = levels // 8
    tiles = ROWS * 144 // LANES
    size, room = share * tiles, slot * tiles
    me = lax.axis_index("lon")
    band = lax.axis_index("lat")
    bands = lax.axis_size("lat")
    west, east = lax.rem(me + PIECES - 1, PIECES), lax.rem(me + 1, PIECES)
    south, north = lax.rem(band + bands - 1, bands), lax.rem(band + 1, bands)
    has_south, has_north = band > 0, band < bands - 1
    lane = lax.broadcasted_iota(jnp.int32, (8, LANES), 1)
    in16 = lane % 16
    sub = lane // 16

    barrier = pltpu.get_barrier_semaphore()
    core = lax.rem(me, 2)
    mate = me + 1 - 2 * core
    for step in range(0, PIECES, 2):
        @pl.when((step > 0) | (core == 1))
        def _():
            pl.semaphore_signal(
                barrier, inc=1, device_id={"lon": lax.rem(me - core + step, PIECES)}, device_id_type=MESH
            )

    load_tan = pltpu.make_async_copy(tan_hbm, tan_v, local_sem.at[0])
    load_wind = pltpu.make_async_copy(wind_hbm, wind_v, local_sem.at[1])
    load_table = pltpu.make_async_copy(table_hbm, table_v, local_sem.at[2])
    own_a = pltpu.make_async_copy(
        adj_hbm.at[pl.ds(me * size, size)], got_a.at[pl.ds(me * room, size)], local_sem.at[4]
    )
    load_tan.start()
    load_wind.start()
    own_a.start()
    load_table.start()

    def tile_of(ref, row, stride=tiles, count=8):
        return ref[pl.ds(row, count, stride=stride), :]

    def pack(source, wind, edge, line):
        planes = fields + (1 if wind is not None else 0)

        def body(lg, carry):
            first, last = list(carry[0]), list(carry[1])
            rest = [jnp.zeros((8, LANES), F32)] * 2
            for f in range(planes):
                if f < fields:
                    at = (f * groups + lg) * 8
                    t = [tile_of(source, at * tiles + k) for k in range(tiles)]
                    line[0, pl.ds(at, 8), :] = t[0]
                    line[1, pl.ds(at, 8), :] = t[tiles - 1]
                    rest[0] = jnp.where(sub == f, pltpu.roll(t[1], 16 * f, 1), rest[0])
                    rest[1] = jnp.where(sub == f, pltpu.roll(t[tiles - 2], 16 * f + 16, 1), rest[1])
                else:
                    t = [tile_of(wind, lg * 8 * tiles + k) for k in range(tiles)]
                    for k in range(2):
                        wind_row[pl.ds(k * levels + lg * 8, 8), :] = tile_of(
                            wind, (groups + lg) * 8 * tiles + k + tiles - 2
                        )
                a, b = t[0], t[1]
                for r in range(1, ROWS):
                    a = jnp.where(sub == r, t[r], a)
                    b = jnp.where(sub == r, t[r + 1], b)
                here = in16 == lg
                first[f] = jnp.where(here, pltpu.roll(a, lg, 1), first[f])
                last[f] = jnp.where(here, pltpu.roll(b, lg + (LANES - 15), 1), last[f])
            for k in range(2):
                line[k, pl.ds(chans + lg * 8, 8), :] = rest[k]
            return tuple(first), tuple(last)

        zero = tuple(jnp.zeros((8, LANES), F32) for _ in range(planes))
        first, last = lax.fori_loop(0, groups, body, (zero, zero))
        for f in range(planes):
            edge[0, 8 * f : 8 * f + 8, :] = first[f]
            edge[1, 8 * f : 8 * f + 8, :] = last[f]

    def edges(edge, at):
        return [
            pltpu.make_async_remote_copy(
                edge.at[0], edge.at[3], edge_send.at[at, 0], edge_recv.at[at, 0],
                device_id={"lon": west}, device_id_type=MESH,
            ),
            pltpu.make_async_remote_copy(
                edge.at[1], edge.at[2], edge_send.at[at, 1], edge_recv.at[at, 1],
                device_id={"lon": east}, device_id_type=MESH,
            ),
        ]

    def rows(line, to_south, to_north, at):
        return [
            pltpu.make_async_remote_copy(
                line.at[0], to_south, row_send.at[at, 0], row_recv.at[at, 0],
                device_id={"lat": south}, device_id_type=MESH,
            ),
            pltpu.make_async_remote_copy(
                line.at[1], to_north, row_send.at[at, 1], row_recv.at[at, 1],
                device_id={"lat": north}, device_id_type=MESH,
            ),
        ]

    def start_rows(copies):
        pl.when(has_south)(copies[0].start)
        pl.when(has_north)(copies[1].start)

    def wait_rows(copies):
        pl.when(has_north)(copies[0].wait_recv)
        pl.when(has_south)(copies[1].wait_recv)

    def sent_rows(copies):
        pl.when(has_south)(copies[0].wait_send)
        pl.when(has_north)(copies[1].wait_send)

    def stencil(source, edge, from_south, from_north, target, sign):
        half_south = jnp.where(has_south, 0.5, 0.0).astype(F32)
        half_north = jnp.where(has_north, 0.5, 0.0).astype(F32)

        def left(x, n):
            return pltpu.roll(x, LANES - n, 1)

        def body(lg, _):
            u = [tile_of(wind_v, lg * 8 * tiles + k) * 0.5 for k in range(tiles)]
            v = [tile_of(wind_v, (groups + lg) * 8 * tiles + k) for k in range(tiles)]
            v = [x * 0.5 for x in v[:-2]] + [v[-2] * jnp.where(lane >= 112, half_north, 0.5), v[-1] * half_north]
            v = [south_w[pl.ds(k * levels + lg * 8, 8), :] * half_south for k in range(2)] + v
            u_west = pltpu.roll(edge_t[2, 8 * fields : 8 * fields + 8, :], LANES - lg, 1) * 0.5
            rest_south = from_south[pl.ds(chans + lg * 8, 8), :]
            rest_north = from_north[pl.ds(chans + lg * 8, 8), :]
            for f in range(fields):
                at = (f * groups + lg) * 8
                t = [tile_of(source, at * tiles + k) for k in range(tiles)]
                far_west = pltpu.roll(edge[2, 8 * f : 8 * f + 8, :], LANES - lg, 1)
                far_east = pltpu.roll(edge[3, 8 * f : 8 * f + 8, :], 15 - lg, 1)
                shifted = [left(x, 1) for x in t]
                flux = []
                for k in range(tiles):
                    nxt = jnp.where(lane == 127, shifted[k + 1], shifted[k]) if k + 1 < tiles else shifted[k]
                    if k >= 1:
                        nxt = jnp.where(lane == 16 * (k - 1) + 15, far_east, nxt)
                    flux.append(u[k] * (t[k] + sign * nxt))
                turned = [pltpu.roll(x, 1, 1) for x in flux]
                out = []
                for k in range(tiles):
                    prev = jnp.where(lane == 0, turned[k - 1], turned[k]) if k >= 1 else turned[k]
                    if k < ROWS:
                        prev = jnp.where(lane == 16 * k, u_west * (far_west + sign * t[k]), prev)
                    out.append(t[k] - flux[k] + sign * prev)
                ext = [pltpu.roll(rest_south, 112 - 16 * f, 1), from_south[pl.ds(at, 8), :]] + t
                ext = ext + [from_north[pl.ds(at, 8), :]]
                shifted = [left(x, 16) for x in ext] + [pltpu.roll(rest_north, 112 - 16 * f, 1)]
                flux = []
                for k in range(tiles + 2):
                    nxt = jnp.where(lane < 112, shifted[k + 1], shifted[k + 2])
                    flux.append(v[k] * (ext[k] + sign * nxt))
                turned = [pltpu.roll(x, 16, 1) for x in flux]
                for k in range(tiles):
                    prev = jnp.where(lane >= 16, turned[k + 1], turned[k])
                    target[pl.ds(at * tiles + k, 8, stride=tiles), :] = out[k] - flux[k + 2] + sign * prev
            return 0

        lax.fori_loop(0, groups, body, 0)

    def matrices():
        grow = lax.broadcasted_iota(jnp.int32, (8, 144), 0)
        limit = jnp.zeros((8, 144), F32)
        for r in range(ROWS):
            limit = jnp.where(grow == r, cut_ref[band * ROWS + r].astype(F32), limit)
        column = lax.broadcasted_iota(jnp.int32, (8, 144), 1)
        nring = PIECES * 144
        part = 0
        for kind in KINDS:
            wave = column * PIECES + kind
            wave = jnp.minimum(wave, jnp.abs(nring - wave)).astype(F32)
            ratio = limit / jnp.maximum(wave, 1.0)
            gain = jnp.where(wave <= limit, 1.0, ratio * ratio)
            high, low = halves(gain)
            both = jnp.concatenate([high, low], axis=0)
            for _ in range(1 if kind in (0, 4) else 2):
                table_high, table_low = halves(table_v[part])
                one = dot(both, table_high)
                two = dot(both, table_low)
                lag_v[part] = one[:8] + one[8:] + two[:8]
                part += 1

        wide = lax.broadcasted_iota(jnp.int32, (16, BLOCK), 1)

        def body(r, _):
            inside = (wide >= 16 * r) & (wide < 16 * r + 144)
            nought = jnp.zeros((16, PIECES * BLOCK), BF16)
            for a in range(9, 16):
                row = lax.rem(r + a, 16) * 16
                mat_high[r, pl.ds(row, 16), :] = nought
                mat_low[r, pl.ds(row, 16), :] = nought
            for part in range(PIECES):
                line = jnp.broadcast_to(lag_v[part, pl.ds(r, 1), :], (16, SPAN))
                strip = pltpu.roll(line, 0, 1, stride=1, stride_axis=0)
                strip = pltpu.roll(strip, 16 * r + (SPAN - 128), 1)
                for a in range(9):
                    block = jnp.where(inside, strip[:, 128 - 16 * a : 384 - 16 * a], 0.0)
                    high, low = halves(block)
                    row = (r + a) * 16
                    mat_high[r, pl.ds(row, 16), part * BLOCK : (part + 1) * BLOCK] = high
                    mat_low[r, pl.ds(row, 16), part * BLOCK : (part + 1) * BLOCK] = low
            return 0

        lax.fori_loop(0, ROWS, body, 0)

    def damp(got, back):
        def forward(p, _):
            for t in range(tiles):
                x = [got[pl.ds(c * room + p * 16 * tiles + t, 16, stride=tiles), :] for c in range(PIECES)]
                for k, y in enumerate(to_parts(x)):
                    high, low = halves(y)
                    part_high[k, pl.ds(p * 16, 16), t * LANES : (t + 1) * LANES] = high
                    part_low[k, pl.ds(p * 16, 16), t * LANES : (t + 1) * LANES] = low
            return 0

        lax.fori_loop(0, slot // 16, forward, 0)
        image_v[:, :, 0:LANES] = jnp.zeros((PIECES, slot, LANES), F32)

        def multiply(r, _):
            window = pl.ds(pl.multiple_of(r * LANES, LANES), BLOCK)
            this = pl.ds(pl.multiple_of(r * LANES, LANES), LANES)
            following = pl.ds(pl.multiple_of(r * LANES + LANES, LANES), LANES)

            def product(first, count):
                high = part_high[first : first + count, :, window].reshape(count * slot, BLOCK)
                low = part_low[first : first + count, :, window].reshape(count * slot, BLOCK)
                cols = slice(first * BLOCK, (first + count) * BLOCK)
                wide_high, wide_low = mat_high[r, :, cols], mat_low[r, :, cols]
                return dot(high, wide_high) + dot(low, wide_high) + dot(high, wide_low)

            def put(k, z):
                image_v[k, :, this] = image_v[k, :, this] + z[:, :LANES]
                image_v[k, :, following] = z[:, LANES:]

            put(0, product(0, 1))
            put(1, product(1, 1))
            for k in (2, 4, 6):
                z = product(k, 2)
                put(k, z[:slot, :BLOCK] - z[slot:, BLOCK:])
                put(k + 1, z[:slot, BLOCK:] + z[slot:, :BLOCK])
            return 0

        lax.fori_loop(0, ROWS, multiply, 0)

        def inverse(p, _):
            for t in range(tiles):
                z = [image_v[k, pl.ds(p * 8, 8), t * LANES : (t + 1) * LANES] for k in range(PIECES)]
                for c, x in enumerate(from_parts(z)):
                    back[pl.ds(c * room + p * 8 * tiles + t, 8, stride=tiles), :] = x
            return 0

        lax.fori_loop(0, slot // 8, inverse, 0)

    def scatter(source, got, send, recv):
        out = []
        for step in ORDER:
            to = lax.rem(me + step, PIECES)
            out.append(
                pltpu.make_async_remote_copy(
                    source.at[pl.ds(to * size, size)], got.at[pl.ds(me * room, size)],
                    send.at[step], recv.at[step], device_id={"lon": to}, device_id_type=MESH,
                )
            )
        return out

    def bring(back, target, send, recv):
        out = []
        for step in ORDER:
            to = lax.rem(me + step, PIECES)
            out.append(
                pltpu.make_async_remote_copy(
                    back.at[pl.ds(to * room, size)], target.at[pl.ds(me * size, size)],
                    send.at[step], recv.at[step], device_id={"lon": to}, device_id_type=MESH,
                )
            )
        return out

    def start(copies):
        for c in copies:
            c.start()

    def wait_recv(copies):
        for c in copies:
            c.wait_recv()

    def wait_send(copies):
        for c in copies:
            c.wait_send()

    @pl.when(core == 0)
    def _():
        pl.semaphore_wait(barrier, PIECES - 1)
        pl.semaphore_signal(cycle_sem, inc=1, device_id={"lon": mate}, device_id_type=MESH)

    @pl.when(core == 1)
    def _():
        pl.semaphore_wait(cycle_sem, 1)
        for there, other in ((has_south, south), (has_north, north)):

            @pl.when(there)
            def _(other=other):
                pl.semaphore_signal(barrier, inc=1, device_id={"lat": other}, device_id_type=MESH)

    @pl.when(band == 0)
    def _():
        south_t[...] = jnp.zeros_like(south_t)
        south_d[...] = jnp.zeros_like(south_d)
        south_w[...] = jnp.zeros_like(south_w)

    @pl.when(band == bands - 1)
    def _():
        north_t[...] = jnp.zeros_like(north_t)
        north_d[...] = jnp.zeros_like(north_d)

    send_a = scatter(adj_hbm, got_a, fwd_a_send, fwd_a_recv)
    start(send_a[:FIRST])
    load_tan.wait()
    load_wind.wait()
    pack(tan_v, wind_v, edge_t, line_t)
    edges_t = edges(edge_t, 0)
    start(edges_t)
    start(send_a[FIRST:])

    @pl.when(core == 1)
    def _():
        pl.semaphore_wait(barrier, jnp.where(has_south & has_north, 2, 1))
        pl.semaphore_signal(bands_sem, inc=1, device_id={"lon": mate}, device_id_type=MESH)

    @pl.when(core == 0)
    def _():
        pl.semaphore_wait(bands_sem, 1)

    rows_t = rows(line_t, north_t, south_t, 0)
    rows_w = pltpu.make_async_remote_copy(
        wind_row, south_w,
        row_send.at[2, 0], row_recv.at[2, 0], device_id={"lat": north}, device_id_type=MESH,
    )
    start_rows(rows_t)
    pl.when(has_north)(rows_w.start)

    wait_recv(edges_t)
    wait_rows(rows_t)
    pl.when(has_south)(rows_w.wait_recv)
    stencil(tan_v, edge_t, south_t, north_t, moved_v, 1.0)
    send_t = scatter(moved_v, got_t, fwd_t_send, fwd_t_recv)
    start(send_t)
    own_t = pltpu.make_async_copy(
        moved_v.at[pl.ds(me * size, size)], got_t.at[pl.ds(me * room, size)], local_sem.at[5]
    )
    own_t.start()

    load_table.wait()
    matrices()
    own_a.wait()
    wait_recv(send_a)
    damp(got_a, back_a)
    home_a = bring(back_a, damped_v, back_a_send, back_a_recv)
    start(home_a)
    keep_a = pltpu.make_async_copy(
        back_a.at[pl.ds(me * room, size)], damped_v.at[pl.ds(me * size, size)], local_sem.at[6]
    )
    keep_a.start()

    own_t.wait()
    wait_recv(send_t)
    damp(got_t, back_t)

    home_t = bring(back_t, tl_out, back_t_send, back_t_recv)
    start(home_t[:FIRST])
    keep_a.wait()
    wait_recv(home_a)
    pack(damped_v, None, edge_d, line_d)
    edges_d = edges(edge_d, 1)
    start(edges_d)
    rows_d = rows(line_d, north_d, south_d, 1)
    start_rows(rows_d)
    start(home_t[FIRST:])
    keep_t = pltpu.make_async_copy(
        back_t.at[pl.ds(me * room, size)], tl_out.at[pl.ds(me * size, size)], local_sem.at[7]
    )
    keep_t.start()

    wait_recv(edges_d)
    wait_rows(rows_d)
    stencil(damped_v, edge_d, south_d, north_d, adj_out, -1.0)

    for copies in (edges_t, send_a, send_t, home_a, edges_d):
        wait_send(copies)
    sent_rows(rows_t)
    sent_rows(rows_d)
    pl.when(has_north)(rows_w.wait_send)
    keep_t.wait()
    for c in home_t:
        c.wait()


def store(tl_ref, adj_ref, tl_out, adj_out, sem):
    rows = tl_ref.shape[0] // PARTS
    copies = []
    for k, (source, target) in enumerate(((tl_ref, tl_out), (adj_ref, adj_out))):
        for p in range(PARTS):
            here = pl.ds(p * rows, rows)
            copies.append(pltpu.make_async_copy(source.at[here], target.at[here], sem.at[k, p]))
    for c in copies:
        c.start()
    for c in copies:
        c.wait()


def shards(tangent, adjoint, winds, cutoff):
    fields, levels, single, cells = tangent.shape
    chans = fields * levels
    share = chans // PIECES
    slot = -(-share // 16) * 16
    tiles = cells // LANES
    table = split_table(PIECES * cells // ROWS)
    any_space = pl.BlockSpec(memory_space=pl.ANY)
    vmem = pltpu.VMEM
    dma = pltpu.SemaphoreType.DMA
    whole = vmem((chans * tiles, LANES), F32)
    tl, adj = pl.pallas_call(
        functools.partial(kernel, (fields, levels, share, slot)),
        out_shape=(whole, whole),
        in_specs=[pl.BlockSpec(memory_space=pltpu.SMEM)] + [any_space] * 4,
        out_specs=(pl.BlockSpec(memory_space=pltpu.VMEM),) * 2,
        scratch_shapes=[
            whole,
            vmem((2 * levels * tiles, LANES), F32),
            whole,
            whole,
            *[vmem((PIECES * slot * tiles, LANES), F32)] * 4,
            *[vmem((chans + levels, LANES), F32)] * 4,
            *[vmem((2 * levels, LANES), F32)] * 2,
            *[vmem((2, chans + levels, LANES), F32)] * 2,
            vmem((4, 8 * (fields + 1), LANES), F32),
            vmem((4, 8 * fields, LANES), F32),
            vmem((PIECES, 144, SPAN), F32),
            vmem((PIECES, ROWS, SPAN), F32),
            vmem((ROWS, BLOCK, PIECES * BLOCK), BF16),
            vmem((ROWS, BLOCK, PIECES * BLOCK), BF16),
            vmem((PIECES, slot, cells), BF16),
            vmem((PIECES, slot, cells), BF16),
            vmem((PIECES, slot, cells), F32),
            dma((8,)),
            *[dma((PIECES,))] * 8,
            dma((2, 2)),
            dma((2, 2)),
            dma((3, 2)),
            dma((3, 2)),
            pltpu.SemaphoreType.REGULAR,
            pltpu.SemaphoreType.REGULAR,
        ],
        compiler_params=pltpu.CompilerParams(
            collective_id=0, has_side_effects=True, vmem_limit_bytes=62600000
        ),
    )(
        cutoff,
        jnp.asarray(table),
        tangent.reshape(chans * tiles, LANES),
        adjoint.reshape(chans * tiles, LANES),
        winds.reshape(2 * levels * tiles, LANES),
    )
    tl, adj = pl.pallas_call(
        store,
        out_shape=(jax.ShapeDtypeStruct((chans * tiles, LANES), F32),) * 2,
        in_specs=[pl.BlockSpec(memory_space=pltpu.VMEM)] * 2,
        out_specs=(any_space, any_space),
        scratch_shapes=[dma((2, PARTS))],
        compiler_params=pltpu.CompilerParams(vmem_limit_bytes=1024 * 1024),
    )(tl, adj)
    return tl.reshape(tangent.shape), adj.reshape(tangent.shape)


def solution(mesh):
    band = P(None, None, "lat", "lon")
    return jax.shard_map(
        shards, mesh=mesh, in_specs=(band, band, band, P()), out_specs=(band, band), check_vma=False
    )
```

```python
import functools
import math

import jax
import jax.numpy as jnp
import numpy as np
from jax import lax
from jax.experimental import pallas as pl
from jax.experimental.pallas import tpu as pltpu
from jax.sharding import PartitionSpec as P

MESH = pl.DeviceIdType.MESH
F32 = jnp.float32
BF16 = jnp.bfloat16
ROWS = 8
PIECES = 8
LANES = 128
BLOCK = 256
SPAN = 512
KINDS = (0, 4, 1, 2, 3)
ORDER = ((1, 0), (3, 0), (2, 0), (2, 1), (1, 1), (3, 1), (0, 1))
NEAR = [k for k, (ahead, _) in enumerate(ORDER) if ahead != 2]
FAR = [k for k, (ahead, _) in enumerate(ORDER) if ahead == 2]
FIRST = 2
PAD = 8
PARTS = 1
ROOT = math.sqrt(0.5)


def split_table(nring):
    lag = np.arange(SPAN) - SPAN // 2
    count = nring // PIECES
    parts = []
    for kind in KINDS:
        wave = kind + PIECES * np.arange(count)
        angle = (wave[:, None] * lag[None, :] % nring) * (2.0 * np.pi / nring)
        forms = (np.cos,) if kind in (0, 4) else (np.cos, np.sin)
        weight = (1.0 if kind in (0, 4) else 2.0) / nring
        for form in forms:
            parts.append(weight * form(angle))
    return np.stack(parts).astype(np.float32)


def halves(value):
    high = value.astype(BF16)
    return high, (value - high.astype(F32)).astype(BF16)


def dot(a, b):
    return jnp.dot(a, b, preferred_element_type=F32)


def to_parts(x):
    s0, d0 = x[0] + x[4], x[0] - x[4]
    s1, d1 = x[1] + x[5], x[1] - x[5]
    s2, d2 = x[2] + x[6], x[2] - x[6]
    s3, d3 = x[3] + x[7], x[3] - x[7]
    even, odd = s0 + s2, s1 + s3
    p, q = (d1 - d3) * ROOT, (d1 + d3) * ROOT
    return (even + odd, even - odd, d0 + p, -d2 - q, s0 - s2, s3 - s1, d0 - p, d2 - q)


def from_parts(z):
    a, b = z[0] + z[1], z[0] - z[1]
    even = (a + z[4], b - z[5], a - z[4], b + z[5])
    p, q = (z[2] - z[6]) * ROOT, (z[3] + z[7]) * ROOT
    odd = (z[2] + z[6], p - q, z[7] - z[3], -p - q)
    return [e + o for e, o in zip(even, odd)] + [e - o for e, o in zip(even, odd)]


def kernel(
    dims,
    cut_ref,
    table_hbm,
    tan_hbm,
    adj_hbm,
    wind_hbm,
    tl_out,
    adj_out,
    tan_v,
    wind_v,
    moved_v,
    damped_v,
    got_a,
    got_t,
    back_a,
    back_t,
    south_t,
    north_t,
    south_d,
    north_d,
    south_w,
    wind_row,
    line_t,
    line_d,
    edge_t,
    edge_d,
    table_v,
    lag_v,
    mat_high,
    mat_low,
    part_high,
    part_low,
    image_v,
    local_sem,
    fwd_a_send,
    fwd_a_recv,
    fwd_t_send,
    fwd_t_recv,
    back_a_send,
    back_a_recv,
    back_t_send,
    back_t_recv,
    edge_send,
    edge_recv,
    row_send,
    row_recv,
    cycle_sem,
    bands_sem,
):
    fields, levels, share, slot = dims
    chans = fields * levels
    groups = levels // 8
    tiles = ROWS * 144 // LANES
    size, room = share * tiles, slot * tiles
    me = lax.axis_index("lon")
    band = lax.axis_index("lat")
    bands = lax.axis_size("lat")
    west, east = lax.rem(me + PIECES - 1, PIECES), lax.rem(me + 1, PIECES)
    south, north = lax.rem(band + bands - 1, bands), lax.rem(band + 1, bands)
    has_south, has_north = band > 0, band < bands - 1
    lane = lax.broadcasted_iota(jnp.int32, (8, LANES), 1)
    in16 = lane % 16
    sub = lane // 16

    barrier = pltpu.get_barrier_semaphore()
    core = lax.rem(me, 2)
    mate = me + 1 - 2 * core

    def device(ahead, flip):
        return lax.rem(me - core + 2 * ahead, PIECES) + (core if flip == 0 else 1 - core)

    def tell(semaphore, axis, other):
        pl.semaphore_signal(semaphore, inc=1, device_id={axis: other}, device_id_type=MESH)

    for ahead in (1, 3):
        tell(barrier, "lon", lax.rem(me - core + 2 * ahead, PIECES))
    tell(barrier, "lon", lax.rem(me - core + 4, PIECES) + 1)
    pl.when(core == 1)(lambda: tell(barrier, "lon", mate))

    load_tan = pltpu.make_async_copy(tan_hbm, tan_v.at[pl.ds(0, chans * tiles)], local_sem.at[0])
    load_wind = pltpu.make_async_copy(wind_hbm, wind_v.at[pl.ds(0, 2 * levels * tiles)], local_sem.at[1])
    load_table = pltpu.make_async_copy(table_hbm, table_v, local_sem.at[2])
    own_a = pltpu.make_async_copy(
        adj_hbm.at[pl.ds(me * size, size)], got_a.at[pl.ds(me * room, size)], local_sem.at[4]
    )
    load_tan.start()
    load_wind.start()
    own_a.start()
    load_table.start()

    def tile_of(ref, row, stride=tiles, count=8):
        return ref[pl.ds(row, count, stride=stride), :]

    def pack(source, wind, edge, line):
        planes = fields + (1 if wind is not None else 0)

        def body(lg, carry):
            first, last = list(carry[0]), list(carry[1])
            rest = [jnp.zeros((8, LANES), F32)] * 2
            for f in range(planes):
                if f < fields:
                    at = (f * groups + lg) * 8
                    t = [tile_of(source, at * tiles + k) for k in range(tiles)]
                    line[0, pl.ds(at, 8), :] = t[0]
                    line[1, pl.ds(at, 8), :] = t[tiles - 1]
                    rest[0] = jnp.where(sub == f, pltpu.roll(t[1], 16 * f, 1), rest[0])
                    rest[1] = jnp.where(sub == f, pltpu.roll(t[tiles - 2], 16 * f + 16, 1), rest[1])
                else:
                    t = [tile_of(wind, lg * 8 * tiles + k) for k in range(tiles)]
                    for k in range(2):
                        wind_row[pl.ds(k * levels + lg * 8, 8), :] = tile_of(
                            wind, (groups + lg) * 8 * tiles + k + tiles - 2
                        )
                a, b = t[0], t[1]
                for r in range(1, ROWS):
                    a = jnp.where(sub == r, t[r], a)
                    b = jnp.where(sub == r, t[r + 1], b)
                here = in16 == lg
                first[f] = jnp.where(here, pltpu.roll(a, lg, 1), first[f])
                last[f] = jnp.where(here, pltpu.roll(b, lg + (LANES - 15), 1), last[f])
            for k in range(2):
                line[k, pl.ds(chans + lg * 8, 8), :] = rest[k]
            return tuple(first), tuple(last)

        zero = tuple(jnp.zeros((8, LANES), F32) for _ in range(planes))
        first, last = lax.fori_loop(0, groups, body, (zero, zero))
        for f in range(planes):
            edge[0, 8 * f : 8 * f + 8, :] = first[f]
            edge[1, 8 * f : 8 * f + 8, :] = last[f]

    def edges(edge, at):
        return [
            pltpu.make_async_remote_copy(
                edge.at[0], edge.at[3], edge_send.at[at, 0], edge_recv.at[at, 0],
                device_id={"lon": west}, device_id_type=MESH,
            ),
            pltpu.make_async_remote_copy(
                edge.at[1], edge.at[2], edge_send.at[at, 1], edge_recv.at[at, 1],
                device_id={"lon": east}, device_id_type=MESH,
            ),
        ]

    def rows(line, to_south, to_north, at):
        return [
            pltpu.make_async_remote_copy(
                line.at[0], to_south, row_send.at[at, 0], row_recv.at[at, 0],
                device_id={"lat": south}, device_id_type=MESH,
            ),
            pltpu.make_async_remote_copy(
                line.at[1], to_north, row_send.at[at, 1], row_recv.at[at, 1],
                device_id={"lat": north}, device_id_type=MESH,
            ),
        ]

    def start_rows(copies):
        pl.when(has_south)(copies[0].start)
        pl.when(has_north)(copies[1].start)

    def wait_rows(copies):
        pl.when(has_north)(copies[0].wait_recv)
        pl.when(has_south)(copies[1].wait_recv)

    def sent_rows(copies):
        pl.when(has_south)(copies[0].wait_send)
        pl.when(has_north)(copies[1].wait_send)

    def stencil(source, edge, from_south, from_north, target, sign):
        half_south = jnp.where(has_south, 0.5, 0.0).astype(F32)
        half_north = jnp.where(has_north, 0.5, 0.0).astype(F32)

        def left(x, n):
            return pltpu.roll(x, LANES - n, 1)

        def body(lg, _):
            u = [tile_of(wind_v, lg * 8 * tiles + k) * 0.5 for k in range(tiles)]
            v = [tile_of(wind_v, (groups + lg) * 8 * tiles + k) for k in range(tiles)]
            v = [x * 0.5 for x in v[:-2]] + [v[-2] * jnp.where(lane >= 112, half_north, 0.5), v[-1] * half_north]
            v = [south_w[pl.ds(k * levels + lg * 8, 8), :] * half_south for k in range(2)] + v
            u_west = pltpu.roll(edge_t[2, 8 * fields : 8 * fields + 8, :], LANES - lg, 1) * 0.5
            rest_south = from_south[pl.ds(chans + lg * 8, 8), :]
            rest_north = from_north[pl.ds(chans + lg * 8, 8), :]
            for f in range(fields):
                at = (f * groups + lg) * 8
                t = [tile_of(source, at * tiles + k) for k in range(tiles)]
                far_west = pltpu.roll(edge[2, 8 * f : 8 * f + 8, :], LANES - lg, 1)
                far_east = pltpu.roll(edge[3, 8 * f : 8 * f + 8, :], 15 - lg, 1)
                shifted = [left(x, 1) for x in t]
                flux = []
                for k in range(tiles):
                    nxt = jnp.where(lane == 127, shifted[k + 1], shifted[k]) if k + 1 < tiles else shifted[k]
                    if k >= 1:
                        nxt = jnp.where(lane == 16 * (k - 1) + 15, far_east, nxt)
                    flux.append(u[k] * (t[k] + sign * nxt))
                turned = [pltpu.roll(x, 1, 1) for x in flux]
                out = []
                for k in range(tiles):
                    prev = jnp.where(lane == 0, turned[k - 1], turned[k]) if k >= 1 else turned[k]
                    if k < ROWS:
                        prev = jnp.where(lane == 16 * k, u_west * (far_west + sign * t[k]), prev)
                    out.append(t[k] - flux[k] + sign * prev)
                ext = [pltpu.roll(rest_south, 112 - 16 * f, 1), from_south[pl.ds(at, 8), :]] + t
                ext = ext + [from_north[pl.ds(at, 8), :]]
                shifted = [left(x, 16) for x in ext] + [pltpu.roll(rest_north, 112 - 16 * f, 1)]
                flux = []
                for k in range(tiles + 2):
                    nxt = jnp.where(lane < 112, shifted[k + 1], shifted[k + 2])
                    flux.append(v[k] * (ext[k] + sign * nxt))
                turned = [pltpu.roll(x, 16, 1) for x in flux]
                for k in range(tiles):
                    prev = jnp.where(lane >= 16, turned[k + 1], turned[k])
                    target[pl.ds(at * tiles + k, 8, stride=tiles), :] = out[k] - flux[k + 2] + sign * prev
            return 0

        lax.fori_loop(0, groups, body, 0)

    def matrices():
        grow = lax.broadcasted_iota(jnp.int32, (8, 144), 0)
        limit = jnp.zeros((8, 144), F32)
        for r in range(ROWS):
            limit = jnp.where(grow == r, cut_ref[band * ROWS + r].astype(F32), limit)
        column = lax.broadcasted_iota(jnp.int32, (8, 144), 1)
        nring = PIECES * 144
        part = 0
        for kind in KINDS:
            wave = column * PIECES + kind
            wave = jnp.minimum(wave, jnp.abs(nring - wave)).astype(F32)
            ratio = limit / jnp.maximum(wave, 1.0)
            gain = jnp.where(wave <= limit, 1.0, ratio * ratio)
            high, low = halves(gain)
            both = jnp.concatenate([high, low], axis=0)
            for _ in range(1 if kind in (0, 4) else 2):
                table_high, table_low = halves(table_v[part])
                one = dot(both, table_high)
                two = dot(both, table_low)
                lag_v[part] = one[:8] + one[8:] + two[:8]
                part += 1

        wide = lax.broadcasted_iota(jnp.int32, (16, BLOCK), 1)

        def body(r, _):
            inside = (wide >= 16 * r) & (wide < 16 * r + 144)
            nought = jnp.zeros((16, PIECES * BLOCK), BF16)
            for a in range(9, 16):
                row = lax.rem(r + a, 16) * 16
                mat_high[r, pl.ds(row, 16), :] = nought
                mat_low[r, pl.ds(row, 16), :] = nought
            for part in range(PIECES):
                line = jnp.broadcast_to(lag_v[part, pl.ds(r, 1), :], (16, SPAN))
                strip = pltpu.roll(line, 0, 1, stride=1, stride_axis=0)
                strip = pltpu.roll(strip, 16 * r + (SPAN - 128), 1)
                for a in range(9):
                    block = jnp.where(inside, strip[:, 128 - 16 * a : 384 - 16 * a], 0.0)
                    high, low = halves(block)
                    row = (r + a) * 16
                    mat_high[r, pl.ds(row, 16), part * BLOCK : (part + 1) * BLOCK] = high
                    mat_low[r, pl.ds(row, 16), part * BLOCK : (part + 1) * BLOCK] = low
            return 0

        lax.fori_loop(0, ROWS, body, 0)

    def damp(got, back):
        def forward(p, _):
            for t in range(tiles):
                x = [got[pl.ds(c * room + p * 16 * tiles + t, 16, stride=tiles), :] for c in range(PIECES)]
                for k, y in enumerate(to_parts(x)):
                    high, low = halves(y)
                    part_high[k, pl.ds(p * 16, 16), t * LANES : (t + 1) * LANES] = high
                    part_low[k, pl.ds(p * 16, 16), t * LANES : (t + 1) * LANES] = low
            return 0

        lax.fori_loop(0, slot // 16, forward, 0)
        image_v[:, :, 0:LANES] = jnp.zeros((PIECES, slot, LANES), F32)

        def multiply(r, _):
            window = pl.ds(pl.multiple_of(r * LANES, LANES), BLOCK)
            this = pl.ds(pl.multiple_of(r * LANES, LANES), LANES)
            following = pl.ds(pl.multiple_of(r * LANES + LANES, LANES), LANES)

            def product(first, count):
                high = part_high[first : first + count, :, window].reshape(count * slot, BLOCK)
                low = part_low[first : first + count, :, window].reshape(count * slot, BLOCK)
                cols = slice(first * BLOCK, (first + count) * BLOCK)
                wide_high, wide_low = mat_high[r, :, cols], mat_low[r, :, cols]
                return dot(high, wide_high) + dot(low, wide_high) + dot(high, wide_low)

            def put(k, z):
                image_v[k, :, this] = image_v[k, :, this] + z[:, :LANES]
                image_v[k, :, following] = z[:, LANES:]

            put(0, product(0, 1))
            put(1, product(1, 1))
            for k in (2, 4, 6):
                z = product(k, 2)
                put(k, z[:slot, :BLOCK] - z[slot:, BLOCK:])
                put(k + 1, z[:slot, BLOCK:] + z[slot:, :BLOCK])
            return 0

        lax.fori_loop(0, ROWS, multiply, 0)

        def inverse(p, _):
            for t in range(tiles):
                z = [image_v[k, pl.ds(p * 8, 8), t * LANES : (t + 1) * LANES] for k in range(PIECES)]
                for c, x in enumerate(from_parts(z)):
                    back[pl.ds(c * room + p * 8 * tiles + t, 8, stride=tiles), :] = x
            return 0

        lax.fori_loop(0, slot // 8, inverse, 0)

    def scatter(source, got, send, recv):
        out = []
        for ahead, flip in ORDER:
            to, step = device(ahead, flip), 2 * ahead + flip
            out.append(
                pltpu.make_async_remote_copy(
                    source.at[pl.ds(to * size, size)], got.at[pl.ds(me * room, size)],
                    send.at[step], recv.at[step], device_id={"lon": to}, device_id_type=MESH,
                )
            )
        return out

    def bring(back, target, send, recv):
        out = []
        for ahead, flip in ORDER:
            to, step = device(ahead, flip), 2 * ahead + flip
            out.append(
                pltpu.make_async_remote_copy(
                    back.at[pl.ds(to * room, size)], target.at[pl.ds(me * size, size)],
                    send.at[step], recv.at[step], device_id={"lon": to}, device_id_type=MESH,
                )
            )
        return out

    def start(copies):
        for c in copies:
            c.start()

    def wait_recv(copies):
        for c in copies:
            c.wait_recv()

    def wait_send(copies):
        for c in copies:
            c.wait_send()

    @pl.when(core == 0)
    def _():
        pl.semaphore_wait(barrier, 5)
        tell(cycle_sem, "lon", mate)

    @pl.when(core == 1)
    def _():
        pl.semaphore_wait(cycle_sem, 1)
        pl.when(has_south)(lambda: tell(barrier, "lat", south))
        pl.when(has_north)(lambda: tell(barrier, "lat", north))

    send_a = scatter(adj_hbm, got_a, fwd_a_send, fwd_a_recv)
    start(send_a[k] for k in NEAR[:2])
    @pl.when(band == 0)
    def _():
        south_t[...] = jnp.zeros_like(south_t)
        south_d[...] = jnp.zeros_like(south_d)
        south_w[...] = jnp.zeros_like(south_w)

    @pl.when(band == bands - 1)
    def _():
        north_t[...] = jnp.zeros_like(north_t)
        north_d[...] = jnp.zeros_like(north_d)

    load_tan.wait()
    load_wind.wait()
    pack(tan_v, wind_v, edge_t, line_t)
    edges_t = edges(edge_t, 0)
    start(edges_t)
    start(send_a[k] for k in NEAR[2:])

    @pl.when(core == 1)
    def _():
        pl.semaphore_wait(barrier, jnp.where(has_south & has_north, 4, 3))
        tell(bands_sem, "lon", mate)

    @pl.when(core == 0)
    def _():
        pl.semaphore_wait(bands_sem, 1)

    start(send_a[k] for k in FAR)
    rows_t = rows(line_t, north_t, south_t, 0)
    rows_w = pltpu.make_async_remote_copy(
        wind_row, south_w,
        row_send.at[2, 0], row_recv.at[2, 0], device_id={"lat": north}, device_id_type=MESH,
    )
    start_rows(rows_t)
    pl.when(has_north)(rows_w.start)

    wait_recv(edges_t)
    wait_rows(rows_t)
    pl.when(has_south)(rows_w.wait_recv)
    stencil(tan_v, edge_t, south_t, north_t, moved_v, 1.0)
    send_t = scatter(moved_v, got_t, fwd_t_send, fwd_t_recv)
    start(send_t)
    own_t = pltpu.make_async_copy(
        moved_v.at[pl.ds(me * size, size)], got_t.at[pl.ds(me * room, size)], local_sem.at[5]
    )
    own_t.start()

    load_table.wait()
    matrices()
    own_a.wait()
    wait_recv(send_a)
    damp(got_a, back_a)
    home_a = bring(back_a, damped_v, back_a_send, back_a_recv)
    start(home_a)
    keep_a = pltpu.make_async_copy(
        back_a.at[pl.ds(me * room, size)], damped_v.at[pl.ds(me * size, size)], local_sem.at[6]
    )
    keep_a.start()

    own_t.wait()
    wait_recv(send_t)
    damp(got_t, back_t)

    home_t = bring(back_t, tl_out, back_t_send, back_t_recv)
    start(home_t[:FIRST])
    keep_a.wait()
    wait_recv(home_a)
    pack(damped_v, None, edge_d, line_d)
    edges_d = edges(edge_d, 1)
    start(edges_d)
    rows_d = rows(line_d, north_d, south_d, 1)
    start_rows(rows_d)
    start(home_t[FIRST:])
    keep_t = pltpu.make_async_copy(
        back_t.at[pl.ds(me * room, size)], tl_out.at[pl.ds(me * size, size)], local_sem.at[7]
    )
    keep_t.start()

    wait_recv(edges_d)
    wait_rows(rows_d)
    stencil(damped_v, edge_d, south_d, north_d, adj_out, -1.0)

    for copies in (edges_t, send_a, send_t, home_a, edges_d):
        wait_send(copies)
    sent_rows(rows_t)
    sent_rows(rows_d)
    pl.when(has_north)(rows_w.wait_send)
    keep_t.wait()
    for c in home_t:
        c.wait()


def store(tl_ref, adj_ref, tl_out, adj_out, sem):
    rows = tl_out.shape[0] // PARTS
    copies = []
    for k, (source, target) in enumerate(((tl_ref, tl_out), (adj_ref, adj_out))):
        for p in range(PARTS):
            here = pl.ds(p * rows, rows)
            copies.append(pltpu.make_async_copy(source.at[here], target.at[here], sem.at[k, p]))
    for c in copies:
        c.start()
    for c in copies:
        c.wait()


def shards(tangent, adjoint, winds, cutoff):
    fields, levels, single, cells = tangent.shape
    chans = fields * levels
    share = chans // PIECES
    slot = -(-share // 16) * 16
    tiles = cells // LANES
    table = split_table(PIECES * cells // ROWS)
    any_space = pl.BlockSpec(memory_space=pl.ANY)
    vmem = pltpu.VMEM
    dma = pltpu.SemaphoreType.DMA
    whole = vmem((chans * tiles + PAD, LANES), F32)
    tl, adj = pl.pallas_call(
        functools.partial(kernel, (fields, levels, share, slot)),
        out_shape=(vmem((chans * tiles, LANES), F32), whole),
        in_specs=[pl.BlockSpec(memory_space=pltpu.SMEM)] + [any_space] * 4,
        out_specs=(pl.BlockSpec(memory_space=pltpu.VMEM),) * 2,
        scratch_shapes=[
            whole,
            vmem((2 * levels * tiles + PAD, LANES), F32),
            whole,
            whole,
            *[vmem((PIECES * slot * tiles + PAD, LANES), F32)] * 4,
            *[vmem((chans + levels, LANES), F32)] * 4,
            *[vmem((2 * levels, LANES), F32)] * 2,
            *[vmem((2, chans + levels, LANES), F32)] * 2,
            vmem((4, 8 * (fields + 1), LANES), F32),
            vmem((4, 8 * fields, LANES), F32),
            vmem((PIECES, 144, SPAN), F32),
            vmem((PIECES, ROWS, SPAN), F32),
            vmem((ROWS, BLOCK, PIECES * BLOCK), BF16),
            vmem((ROWS, BLOCK, PIECES * BLOCK), BF16),
            vmem((PIECES, slot, cells), BF16),
            vmem((PIECES, slot, cells), BF16),
            vmem((PIECES, slot, cells), F32),
            dma((8,)),
            *[dma((PIECES,))] * 8,
            dma((2, 2)),
            dma((2, 2)),
            dma((3, 2)),
            dma((3, 2)),
            pltpu.SemaphoreType.REGULAR,
            pltpu.SemaphoreType.REGULAR,
        ],
        compiler_params=pltpu.CompilerParams(
            collective_id=0, has_side_effects=True, vmem_limit_bytes=62600000
        ),
    )(
        cutoff,
        jnp.asarray(table),
        tangent.reshape(chans * tiles, LANES),
        adjoint.reshape(chans * tiles, LANES),
        winds.reshape(2 * levels * tiles, LANES),
    )
    tl, adj = pl.pallas_call(
        store,
        out_shape=(jax.ShapeDtypeStruct((chans * tiles, LANES), F32),) * 2,
        in_specs=[pl.BlockSpec(memory_space=pltpu.VMEM)] * 2,
        out_specs=(any_space, any_space),
        scratch_shapes=[dma((2, PARTS))],
        compiler_params=pltpu.CompilerParams(vmem_limit_bytes=1024 * 1024),
    )(tl, adj)
    return tl.reshape(tangent.shape), adj.reshape(tangent.shape)


def solution(mesh):
    band = P(None, None, "lat", "lon")
    return jax.shard_map(
        shards, mesh=mesh, in_specs=(band, band, band, P()), out_specs=(band, band), check_vma=False
    )
```

```python
import functools
import math

import jax
import jax.numpy as jnp
import numpy as np
from jax import lax
from jax.experimental import pallas as pl
from jax.experimental.pallas import tpu as pltpu
from jax.sharding import PartitionSpec as P

MESH = pl.DeviceIdType.MESH
F32 = jnp.float32
BF16 = jnp.bfloat16
ROWS = 8
PIECES = 8
LANES = 128
BLOCK = 256
SPAN = 512
KINDS = (0, 4, 1, 2, 3)
ORDER = ((1, 0), (3, 0), (2, 0), (2, 1), (1, 1), (3, 1), (0, 1))
NEAR = [k for k, (ahead, _) in enumerate(ORDER) if ahead != 2]
FAR = [k for k, (ahead, _) in enumerate(ORDER) if ahead == 2]
FIRST = 2
PAD = 8
PARTS = 1
ROOT = math.sqrt(0.5)


def split_table(nring):
    lag = np.arange(SPAN) - SPAN // 2
    count = nring // PIECES
    parts = []
    for kind in KINDS:
        wave = kind + PIECES * np.arange(count)
        angle = (wave[:, None] * lag[None, :] % nring) * (2.0 * np.pi / nring)
        forms = (np.cos,) if kind in (0, 4) else (np.cos, np.sin)
        weight = (1.0 if kind in (0, 4) else 2.0) / nring
        for form in forms:
            parts.append(weight * form(angle))
    return np.stack(parts).astype(np.float32)


def halves(value):
    high = value.astype(BF16)
    return high, (value - high.astype(F32)).astype(BF16)


def dot(a, b):
    return jnp.dot(a, b, preferred_element_type=F32)


def to_parts(x):
    s0, d0 = x[0] + x[4], x[0] - x[4]
    s1, d1 = x[1] + x[5], x[1] - x[5]
    s2, d2 = x[2] + x[6], x[2] - x[6]
    s3, d3 = x[3] + x[7], x[3] - x[7]
    even, odd = s0 + s2, s1 + s3
    p, q = (d1 - d3) * ROOT, (d1 + d3) * ROOT
    return (even + odd, even - odd, d0 + p, -d2 - q, s0 - s2, s3 - s1, d0 - p, d2 - q)


def from_parts(z):
    a, b = z[0] + z[1], z[0] - z[1]
    even = (a + z[4], b - z[5], a - z[4], b + z[5])
    p, q = (z[2] - z[6]) * ROOT, (z[3] + z[7]) * ROOT
    odd = (z[2] + z[6], p - q, z[7] - z[3], -p - q)
    return [e + o for e, o in zip(even, odd)] + [e - o for e, o in zip(even, odd)]


def kernel(
    dims,
    cut_ref,
    table_hbm,
    tan_hbm,
    adj_hbm,
    wind_hbm,
    tl_out,
    adj_out,
    tan_v,
    wind_v,
    moved_v,
    damped_v,
    got_a,
    got_t,
    back_a,
    back_t,
    south_t,
    north_t,
    south_d,
    north_d,
    south_w,
    wind_row,
    line_t,
    line_d,
    edge_t,
    edge_d,
    table_v,
    lag_v,
    mat_high,
    mat_low,
    part_high,
    part_low,
    image_v,
    local_sem,
    fwd_a_send,
    fwd_a_recv,
    fwd_t_send,
    fwd_t_recv,
    back_a_send,
    back_a_recv,
    back_t_send,
    back_t_recv,
    edge_send,
    edge_recv,
    row_send,
    row_recv,
    cycle_sem,
    bands_sem,
):
    fields, levels, share, slot = dims
    chans = fields * levels
    groups = levels // 8
    tiles = ROWS * 144 // LANES
    size, room = share * tiles, slot * tiles
    me = lax.axis_index("lon")
    band = lax.axis_index("lat")
    bands = lax.axis_size("lat")
    west, east = lax.rem(me + PIECES - 1, PIECES), lax.rem(me + 1, PIECES)
    south, north = lax.rem(band + bands - 1, bands), lax.rem(band + 1, bands)
    has_south, has_north = band > 0, band < bands - 1
    lane = lax.broadcasted_iota(jnp.int32, (8, LANES), 1)
    in16 = lane % 16
    sub = lane // 16

    barrier = pltpu.get_barrier_semaphore()
    core = lax.rem(me, 2)
    mate = me + 1 - 2 * core

    def device(ahead, flip):
        return lax.rem(me - core + 2 * ahead, PIECES) + (core if flip == 0 else 1 - core)

    def tell(semaphore, axis, other):
        pl.semaphore_signal(semaphore, inc=1, device_id={axis: other}, device_id_type=MESH)

    for ahead in (1, 3):
        tell(barrier, "lon", lax.rem(me - core + 2 * ahead, PIECES))
    tell(barrier, "lon", lax.rem(me - core + 4, PIECES) + 1)
    pl.when(core == 1)(lambda: tell(barrier, "lon", mate))

    load_tan = pltpu.make_async_copy(tan_hbm, tan_v.at[pl.ds(0, chans * tiles)], local_sem.at[0])
    load_wind = pltpu.make_async_copy(wind_hbm, wind_v.at[pl.ds(0, 2 * levels * tiles)], local_sem.at[1])
    load_table = pltpu.make_async_copy(table_hbm, table_v, local_sem.at[2])
    own_a = pltpu.make_async_copy(
        adj_hbm.at[pl.ds(me * size, size)], got_a.at[pl.ds(me * room, size)], local_sem.at[4]
    )
    load_tan.start()
    load_wind.start()
    own_a.start()
    load_table.start()

    def tile_of(ref, row, stride=tiles, count=8):
        return ref[pl.ds(row, count, stride=stride), :]

    def pack(source, wind, edge, line):
        planes = fields + (1 if wind is not None else 0)

        def body(lg, carry):
            first, last = list(carry[0]), list(carry[1])
            rest = [jnp.zeros((8, LANES), F32)] * 2
            for f in range(planes):
                if f < fields:
                    at = (f * groups + lg) * 8
                    t = [tile_of(source, at * tiles + k) for k in range(tiles)]
                    line[0, pl.ds(at, 8), :] = t[0]
                    line[1, pl.ds(at, 8), :] = t[tiles - 1]
                    rest[0] = jnp.where(sub == f, pltpu.roll(t[1], 16 * f, 1), rest[0])
                    rest[1] = jnp.where(sub == f, pltpu.roll(t[tiles - 2], 16 * f + 16, 1), rest[1])
                else:
                    t = [tile_of(wind, lg * 8 * tiles + k) for k in range(tiles)]
                    for k in range(2):
                        wind_row[pl.ds(k * levels + lg * 8, 8), :] = tile_of(
                            wind, (groups + lg) * 8 * tiles + k + tiles - 2
                        )
                a, b = t[0], t[1]
                for r in range(1, ROWS):
                    a = jnp.where(sub == r, t[r], a)
                    b = jnp.where(sub == r, t[r + 1], b)
                here = in16 == lg
                first[f] = jnp.where(here, pltpu.roll(a, lg, 1), first[f])
                last[f] = jnp.where(here, pltpu.roll(b, lg + (LANES - 15), 1), last[f])
            for k in range(2):
                line[k, pl.ds(chans + lg * 8, 8), :] = rest[k]
            return tuple(first), tuple(last)

        zero = tuple(jnp.zeros((8, LANES), F32) for _ in range(planes))
        first, last = lax.fori_loop(0, groups, body, (zero, zero))
        for f in range(planes):
            edge[0, 8 * f : 8 * f + 8, :] = first[f]
            edge[1, 8 * f : 8 * f + 8, :] = last[f]

    def edges(edge, at):
        return [
            pltpu.make_async_remote_copy(
                edge.at[0], edge.at[3], edge_send.at[at, 0], edge_recv.at[at, 0],
                device_id={"lon": west}, device_id_type=MESH,
            ),
            pltpu.make_async_remote_copy(
                edge.at[1], edge.at[2], edge_send.at[at, 1], edge_recv.at[at, 1],
                device_id={"lon": east}, device_id_type=MESH,
            ),
        ]

    def rows(line, to_south, to_north, at):
        return [
            pltpu.make_async_remote_copy(
                line.at[0], to_south, row_send.at[at, 0], row_recv.at[at, 0],
                device_id={"lat": south}, device_id_type=MESH,
            ),
            pltpu.make_async_remote_copy(
                line.at[1], to_north, row_send.at[at, 1], row_recv.at[at, 1],
                device_id={"lat": north}, device_id_type=MESH,
            ),
        ]

    def start_rows(copies):
        pl.when(has_south)(copies[0].start)
        pl.when(has_north)(copies[1].start)

    def wait_rows(copies):
        pl.when(has_north)(copies[0].wait_recv)
        pl.when(has_south)(copies[1].wait_recv)

    def sent_rows(copies):
        pl.when(has_south)(copies[0].wait_send)
        pl.when(has_north)(copies[1].wait_send)

    def stencil(source, edge, from_south, from_north, target, sign):
        half_south = jnp.where(has_south, 0.5, 0.0).astype(F32)
        half_north = jnp.where(has_north, 0.5, 0.0).astype(F32)

        def left(x, n):
            return pltpu.roll(x, LANES - n, 1)

        def body(lg, _):
            u = [tile_of(wind_v, lg * 8 * tiles + k) * 0.5 for k in range(tiles)]
            v = [tile_of(wind_v, (groups + lg) * 8 * tiles + k) for k in range(tiles)]
            v = [x * 0.5 for x in v[:-2]] + [v[-2] * jnp.where(lane >= 112, half_north, 0.5), v[-1] * half_north]
            v = [south_w[pl.ds(k * levels + lg * 8, 8), :] * half_south for k in range(2)] + v
            u_west = pltpu.roll(edge_t[2, 8 * fields : 8 * fields + 8, :], LANES - lg, 1) * 0.5
            rest_south = from_south[pl.ds(chans + lg * 8, 8), :]
            rest_north = from_north[pl.ds(chans + lg * 8, 8), :]
            for f in range(fields):
                at = (f * groups + lg) * 8
                t = [tile_of(source, at * tiles + k) for k in range(tiles)]
                far_west = pltpu.roll(edge[2, 8 * f : 8 * f + 8, :], LANES - lg, 1)
                far_east = pltpu.roll(edge[3, 8 * f : 8 * f + 8, :], 15 - lg, 1)
                shifted = [left(x, 1) for x in t]
                flux = []
                for k in range(tiles):
                    nxt = jnp.where(lane == 127, shifted[k + 1], shifted[k]) if k + 1 < tiles else shifted[k]
                    if k >= 1:
                        nxt = jnp.where(lane == 16 * (k - 1) + 15, far_east, nxt)
                    flux.append(u[k] * (t[k] + sign * nxt))
                turned = [pltpu.roll(x, 1, 1) for x in flux]
                out = []
                for k in range(tiles):
                    prev = jnp.where(lane == 0, turned[k - 1], turned[k]) if k >= 1 else turned[k]
                    if k < ROWS:
                        prev = jnp.where(lane == 16 * k, u_west * (far_west + sign * t[k]), prev)
                    out.append(t[k] - flux[k] + sign * prev)
                ext = [pltpu.roll(rest_south, 112 - 16 * f, 1), from_south[pl.ds(at, 8), :]] + t
                ext = ext + [from_north[pl.ds(at, 8), :]]
                shifted = [left(x, 16) for x in ext] + [pltpu.roll(rest_north, 112 - 16 * f, 1)]
                flux = []
                for k in range(tiles + 2):
                    nxt = jnp.where(lane < 112, shifted[k + 1], shifted[k + 2])
                    flux.append(v[k] * (ext[k] + sign * nxt))
                turned = [pltpu.roll(x, 16, 1) for x in flux]
                for k in range(tiles):
                    prev = jnp.where(lane >= 16, turned[k + 1], turned[k])
                    target[pl.ds(at * tiles + k, 8, stride=tiles), :] = out[k] - flux[k + 2] + sign * prev
            return 0

        lax.fori_loop(0, groups, body, 0)

    def matrices():
        grow = lax.broadcasted_iota(jnp.int32, (8, 144), 0)
        limit = jnp.zeros((8, 144), F32)
        for r in range(ROWS):
            limit = jnp.where(grow == r, cut_ref[band * ROWS + r].astype(F32), limit)
        column = lax.broadcasted_iota(jnp.int32, (8, 144), 1)
        nring = PIECES * 144
        part = 0
        for kind in KINDS:
            wave = column * PIECES + kind
            wave = jnp.minimum(wave, jnp.abs(nring - wave)).astype(F32)
            ratio = limit / jnp.maximum(wave, 1.0)
            gain = jnp.where(wave <= limit, 1.0, ratio * ratio)
            high, low = halves(gain)
            both = jnp.concatenate([high, low], axis=0)
            for _ in range(1 if kind in (0, 4) else 2):
                table_high, table_low = halves(table_v[part])
                one = dot(both, table_high)
                two = dot(both, table_low)
                lag_v[part] = one[:8] + one[8:] + two[:8]
                part += 1

        wide = lax.broadcasted_iota(jnp.int32, (16, BLOCK), 1)

        def body(r, _):
            inside = (wide >= 16 * r) & (wide < 16 * r + 144)
            nought = jnp.zeros((16, PIECES * BLOCK), BF16)
            for a in range(9, 16):
                row = lax.rem(r + a, 16) * 16
                mat_high[r, pl.ds(row, 16), :] = nought
                mat_low[r, pl.ds(row, 16), :] = nought
            for part in range(PIECES):
                line = jnp.broadcast_to(lag_v[part, pl.ds(r, 1), :], (16, SPAN))
                strip = pltpu.roll(line, 0, 1, stride=1, stride_axis=0)
                strip = pltpu.roll(strip, 16 * r + (SPAN - 128), 1)
                for a in range(9):
                    block = jnp.where(inside, strip[:, 128 - 16 * a : 384 - 16 * a], 0.0)
                    high, low = halves(block)
                    row = (r + a) * 16
                    mat_high[r, pl.ds(row, 16), part * BLOCK : (part + 1) * BLOCK] = high
                    mat_low[r, pl.ds(row, 16), part * BLOCK : (part + 1) * BLOCK] = low
            return 0

        lax.fori_loop(0, ROWS, body, 0)

    def damp(got, back):
        def forward(p, _):
            for t in range(tiles):
                x = [got[pl.ds(c * room + p * 16 * tiles + t, 16, stride=tiles), :] for c in range(PIECES)]
                for k, y in enumerate(to_parts(x)):
                    high, low = halves(y)
                    part_high[k, pl.ds(p * 16, 16), t * LANES : (t + 1) * LANES] = high
                    part_low[k, pl.ds(p * 16, 16), t * LANES : (t + 1) * LANES] = low
            return 0

        lax.fori_loop(0, slot // 16, forward, 0)
        image_v[:, :, 0:LANES] = jnp.zeros((PIECES, slot, LANES), F32)

        def multiply(r, _):
            window = pl.ds(pl.multiple_of(r * LANES, LANES), BLOCK)
            this = pl.ds(pl.multiple_of(r * LANES, LANES), LANES)
            following = pl.ds(pl.multiple_of(r * LANES + LANES, LANES), LANES)

            def product(first, count):
                high = part_high[first : first + count, :, window].reshape(count * slot, BLOCK)
                low = part_low[first : first + count, :, window].reshape(count * slot, BLOCK)
                cols = slice(first * BLOCK, (first + count) * BLOCK)
                wide_high, wide_low = mat_high[r, :, cols], mat_low[r, :, cols]
                return dot(high, wide_high) + dot(low, wide_high) + dot(high, wide_low)

            def put(k, z):
                image_v[k, :, this] = image_v[k, :, this] + z[:, :LANES]
                image_v[k, :, following] = z[:, LANES:]

            put(0, product(0, 1))
            put(1, product(1, 1))
            for k in (2, 4, 6):
                z = product(k, 2)
                put(k, z[:slot, :BLOCK] - z[slot:, BLOCK:])
                put(k + 1, z[:slot, BLOCK:] + z[slot:, :BLOCK])
            return 0

        lax.fori_loop(0, ROWS, multiply, 0)

        def inverse(p, _):
            for t in range(tiles):
                z = [image_v[k, pl.ds(p * 8, 8), t * LANES : (t + 1) * LANES] for k in range(PIECES)]
                for c, x in enumerate(from_parts(z)):
                    back[pl.ds(c * room + p * 8 * tiles + t, 8, stride=tiles), :] = x
            return 0

        lax.fori_loop(0, slot // 8, inverse, 0)

    def scatter(source, got, send, recv):
        out = []
        for ahead, flip in ORDER:
            to, step = device(ahead, flip), 2 * ahead + flip
            out.append(
                pltpu.make_async_remote_copy(
                    source.at[pl.ds(to * size, size)], got.at[pl.ds(me * room, size)],
                    send.at[step], recv.at[step], device_id={"lon": to}, device_id_type=MESH,
                )
            )
        return out

    def bring(back, target, send, recv):
        out = []
        for ahead, flip in ORDER:
            to, step = device(ahead, flip), 2 * ahead + flip
            out.append(
                pltpu.make_async_remote_copy(
                    back.at[pl.ds(to * room, size)], target.at[pl.ds(me * size, size)],
                    send.at[step], recv.at[step], device_id={"lon": to}, device_id_type=MESH,
                )
            )
        return out

    def start(copies):
        for c in copies:
            c.start()

    def wait_recv(copies):
        for c in copies:
            c.wait_recv()

    def wait_send(copies):
        for c in copies:
            c.wait_send()

    @pl.when(band == 0)
    def _():
        south_t[...] = jnp.zeros_like(south_t)
        south_d[...] = jnp.zeros_like(south_d)
        south_w[...] = jnp.zeros_like(south_w)

    @pl.when(band == bands - 1)
    def _():
        north_t[...] = jnp.zeros_like(north_t)
        north_d[...] = jnp.zeros_like(north_d)

    @pl.when(core == 0)
    def _():
        pl.semaphore_wait(barrier, 5)
        tell(cycle_sem, "lon", mate)

    @pl.when(core == 1)
    def _():
        pl.semaphore_wait(cycle_sem, 1)
        pl.when(has_south)(lambda: tell(barrier, "lat", south))
        pl.when(has_north)(lambda: tell(barrier, "lat", north))

    send_a = scatter(adj_hbm, got_a, fwd_a_send, fwd_a_recv)
    start(send_a[k] for k in NEAR[:2])
    load_tan.wait()
    load_wind.wait()
    pack(tan_v, wind_v, edge_t, line_t)
    edges_t = edges(edge_t, 0)
    start(edges_t)
    start(send_a[k] for k in NEAR[2:])

    @pl.when(core == 1)
    def _():
        pl.semaphore_wait(barrier, jnp.where(has_south & has_north, 4, 3))
        tell(bands_sem, "lon", mate)

    @pl.when(core == 0)
    def _():
        pl.semaphore_wait(bands_sem, 1)

    start(send_a[k] for k in FAR)
    rows_t = rows(line_t, north_t, south_t, 0)
    rows_w = pltpu.make_async_remote_copy(
        wind_row, south_w,
        row_send.at[2, 0], row_recv.at[2, 0], device_id={"lat": north}, device_id_type=MESH,
    )
    start_rows(rows_t)
    pl.when(has_north)(rows_w.start)

    wait_recv(edges_t)
    wait_rows(rows_t)
    pl.when(has_south)(rows_w.wait_recv)
    stencil(tan_v, edge_t, south_t, north_t, moved_v, 1.0)
    send_t = scatter(moved_v, got_t, fwd_t_send, fwd_t_recv)
    start(send_t)
    own_t = pltpu.make_async_copy(
        moved_v.at[pl.ds(me * size, size)], got_t.at[pl.ds(me * room, size)], local_sem.at[5]
    )
    own_t.start()

    load_table.wait()
    matrices()
    own_a.wait()
    wait_recv(send_a)
    damp(got_a, back_a)
    home_a = bring(back_a, damped_v, back_a_send, back_a_recv)
    start(home_a)
    keep_a = pltpu.make_async_copy(
        back_a.at[pl.ds(me * room, size)], damped_v.at[pl.ds(me * size, size)], local_sem.at[6]
    )
    keep_a.start()

    own_t.wait()
    wait_recv(send_t)
    damp(got_t, back_t)

    home_t = bring(back_t, tl_out, back_t_send, back_t_recv)
    start(home_t[:FIRST])
    keep_a.wait()
    wait_recv(home_a)
    pack(damped_v, None, edge_d, line_d)
    edges_d = edges(edge_d, 1)
    start(edges_d)
    rows_d = rows(line_d, north_d, south_d, 1)
    start_rows(rows_d)
    start(home_t[FIRST:])
    keep_t = pltpu.make_async_copy(
        back_t.at[pl.ds(me * room, size)], tl_out.at[pl.ds(me * size, size)], local_sem.at[7]
    )
    keep_t.start()

    wait_recv(edges_d)
    wait_rows(rows_d)
    stencil(damped_v, edge_d, south_d, north_d, adj_out, -1.0)

    for copies in (edges_t, send_a, send_t, home_a, edges_d):
        wait_send(copies)
    sent_rows(rows_t)
    sent_rows(rows_d)
    pl.when(has_north)(rows_w.wait_send)
    keep_t.wait()
    for c in home_t:
        c.wait()


def store(tl_ref, adj_ref, tl_out, adj_out, sem):
    rows = tl_out.shape[0] // PARTS
    copies = []
    for k, (source, target) in enumerate(((tl_ref, tl_out), (adj_ref, adj_out))):
        for p in range(PARTS):
            here = pl.ds(p * rows, rows)
            copies.append(pltpu.make_async_copy(source.at[here], target.at[here], sem.at[k, p]))
    for c in copies:
        c.start()
    for c in copies:
        c.wait()


def shards(tangent, adjoint, winds, cutoff):
    fields, levels, single, cells = tangent.shape
    chans = fields * levels
    share = chans // PIECES
    slot = -(-share // 16) * 16
    tiles = cells // LANES
    table = split_table(PIECES * cells // ROWS)
    any_space = pl.BlockSpec(memory_space=pl.ANY)
    vmem = pltpu.VMEM
    dma = pltpu.SemaphoreType.DMA
    whole = vmem((chans * tiles + PAD, LANES), F32)
    tl, adj = pl.pallas_call(
        functools.partial(kernel, (fields, levels, share, slot)),
        out_shape=(vmem((chans * tiles, LANES), F32), whole),
        in_specs=[pl.BlockSpec(memory_space=pltpu.SMEM)] + [any_space] * 4,
        out_specs=(pl.BlockSpec(memory_space=pltpu.VMEM),) * 2,
        scratch_shapes=[
            whole,
            vmem((2 * levels * tiles + PAD, LANES), F32),
            whole,
            whole,
            *[vmem((PIECES * slot * tiles + PAD, LANES), F32)] * 4,
            *[vmem((chans + levels, LANES), F32)] * 4,
            *[vmem((2 * levels, LANES), F32)] * 2,
            *[vmem((2, chans + levels, LANES), F32)] * 2,
            vmem((4, 8 * (fields + 1), LANES), F32),
            vmem((4, 8 * fields, LANES), F32),
            vmem((PIECES, 144, SPAN), F32),
            vmem((PIECES, ROWS, SPAN), F32),
            vmem((ROWS, BLOCK, PIECES * BLOCK), BF16),
            vmem((ROWS, BLOCK, PIECES * BLOCK), BF16),
            vmem((PIECES, slot, cells), BF16),
            vmem((PIECES, slot, cells), BF16),
            vmem((PIECES, slot, cells), F32),
            dma((8,)),
            *[dma((PIECES,))] * 8,
            dma((2, 2)),
            dma((2, 2)),
            dma((3, 2)),
            dma((3, 2)),
            pltpu.SemaphoreType.REGULAR,
            pltpu.SemaphoreType.REGULAR,
        ],
        compiler_params=pltpu.CompilerParams(
            collective_id=0, has_side_effects=True, vmem_limit_bytes=62600000
        ),
    )(
        cutoff,
        jnp.asarray(table),
        tangent.reshape(chans * tiles, LANES),
        adjoint.reshape(chans * tiles, LANES),
        winds.reshape(2 * levels * tiles, LANES),
    )
    tl, adj = pl.pallas_call(
        store,
        out_shape=(jax.ShapeDtypeStruct((chans * tiles, LANES), F32),) * 2,
        in_specs=[pl.BlockSpec(memory_space=pltpu.VMEM)] * 2,
        out_specs=(any_space, any_space),
        scratch_shapes=[dma((2, PARTS))],
        compiler_params=pltpu.CompilerParams(vmem_limit_bytes=1024 * 1024),
    )(tl, adj)
    return tl.reshape(tangent.shape), adj.reshape(tangent.shape)


def solution(mesh):
    band = P(None, None, "lat", "lon")
    return jax.shard_map(
        shards, mesh=mesh, in_specs=(band, band, band, P()), out_specs=(band, band), check_vma=False
    )
```
